32 devices in a mesh: groups: 2 (over y), flat: 4 (over z), dp: 4 (over x, core).
Axes of the slice: x: 2, y: 2, z: 4, core: 2. Of those that a mesh axis runs over, the one named last changes fastest.
Arguments:
- activations: bfloat16 [4096, 14336], P(('groups', 'dp'), 'flat'), parts along dimension 0
- curvature: float32 [4096], P(('groups', 'dp')), parts along dimension 0, may hold values from 0.3 to 3
- vector_now: float32 [28672, 4096], P(('groups', 'flat', 'dp')), parts along dimension 0
- vector_before: float32 [28672, 4096], P(('groups', 'flat', 'dp')), parts along dimension 0, may hold values from -6 to 6
- sign_bits: int32 [28672, 4096], P(('groups', 'flat', 'dp')), parts along dimension 0, may hold values from 0 to 1
- prior_precision: float32 [2], P('groups'), parts along dimension 0, may hold values from 0.2 to 2
- beta_before: float32 [2], P('groups'), parts along dimension 0, may hold values from 0.3 to 1.5
- kept_rows: int32 [8192], P('groups'), parts along dimension 0, may hold values from 0 to 3583
- kept_cols: int32 [8192], P('groups'), parts along dimension 0, may hold values from 0 to 16383
Outputs:
- vector_next: float32 [28672, 4096], P(('groups', 'flat', 'dp')), parts along dimension 0
- alpha_value: float32 [2], P('groups'), parts along dimension 0
- beta_value: float32 [2], P('groups'), parts along dimension 0
- sketch: float32 [8192], P('groups'), parts along dimension 0
The draws below stay inside these ranges and needn't reach their ends.
There are 2 independent parts, one for each index of `groups`. The reference program is written for one: setup_inputs(seed, part) draws one part's arguments, and reference() takes and returns one part's arrays. A program takes and returns all parts, laid end to end along the dimension named above; each array names one. Nothing has to cross between parts.
All inputs are finite; a program needn't handle non-finite values.
Results may differ from the reference program's by a relative error of at most 0.015.
Values may be sent and summed in bfloat16 or wider, within the bound.
A program may use at most 256 MiB of HBM per device.

```python
import math
import jax
import jax.numpy as jnp
from jax import lax

FF = 14336
D = 4096
TOK_DEV = 512
BLOCK = 128
KEPT = 4096
TOKENS = 2048
NA = 3584
N_FLAT = 4
N_DP = 4


def draw_activations(key, part):
    key_random = jax.random.fold_in(key, 11)
    key_spread = jax.random.fold_in(key, 12)
    growth = 3.0 ** (jnp.arange(FF, dtype=jnp.float32) / FF)
    spread = 10.0 ** jax.random.uniform(key_spread, (FF,), jnp.float32)
    values = jnp.clip(jax.random.normal(key_random, (TOKENS, FF), jnp.float32), -6.0, 6.0)
    return (0.1 * values * spread * growth).astype(jnp.bfloat16)


def draw_vector_now(key, part):
    key_random = jax.random.fold_in(key, 21)
    key_spread = jax.random.fold_in(key, 22)
    spread = 0.25 * 10.0 ** jax.random.uniform(key_spread, (1, D), jnp.float32)
    values = jnp.clip(jax.random.normal(key_random, (FF, D), jnp.float32), -6.0, 6.0)
    return values * spread


def set_ends(entries, own_key, least, largest):
    dims = entries.shape
    place = [jax.random.randint(jax.random.fold_in(own_key, axis), (), 0, dims[axis]) for axis in range(len(dims))]
    entries = entries.at[tuple(place)].set(least)
    longest = dims.index(max(dims))
    place[longest] = (place[longest] + 1) % dims[longest]
    return entries.at[tuple(place)].set(largest)


def levels(key, extent, split, least, top_value):
    def one(dim, blocks):
        draws = jax.random.uniform(jax.random.fold_in(jax.random.fold_in(key, 6), dim), (blocks,), jnp.float32, least / len(split), top_value / len(split))
        return jnp.repeat(jnp.exp(draws), extent[dim] // blocks).reshape((-1,) + (1,) * (len(extent) - dim - 1))

    factor_of = one(*split[0])
    for cut in split[1:]:
        factor_of = factor_of * one(*cut)
    return factor_of


def scatter_about(rng, extent, width, bound, cuts=(), kind=jnp.bfloat16):
    factor_of = levels(rng, extent, cuts, -0.22, 0.18) if cuts else 1.0
    array = jax.random.normal(rng, extent, jnp.float32) * width * factor_of
    return jnp.minimum(jnp.maximum(array, -bound), bound).astype(kind)


def setup_inputs(seed: int = 0, part: int = 0) -> dict:
    splits = jax.random.split(jax.random.key(seed), 10)
    part_splits = jax.random.split(jax.random.fold_in(splits[9], part), 10)
    return {
        "activations": draw_activations(jax.random.fold_in(jax.random.fold_in(splits[9], part), 71), part),
        "curvature": jnp.clip(jnp.exp(math.log(3.0) - 2.3025851 * jax.random.uniform(part_splits[1], (TOKENS,), jnp.float32) ** levels(part_splits[1], (TOKENS,), ((0, 4),), -0.2, 0.2)), 0.3, 3.0),
        "vector_now": draw_vector_now(jax.random.fold_in(jax.random.fold_in(splits[9], part), 71), part),
        "vector_before": scatter_about(part_splits[3], (FF, D), 1.0, 6.0, ((0, 16),), jnp.float32),
        "sign_bits": set_ends(jax.random.randint(part_splits[4], (FF, D), 0, 2), jax.random.fold_in(part_splits[4], 1), 0, 1).astype(jnp.int32),
        "prior_precision": jnp.clip(jnp.exp(jax.random.uniform(part_splits[5], (1,), jnp.float32, math.log(0.2), math.log(2.0))), 0.2, 2.0),
        "beta_before": jnp.clip(jnp.exp(jax.random.uniform(part_splits[6], (1,), jnp.float32, math.log(0.3), math.log(1.5))), 0.3, 1.5),
        "kept_rows": set_ends(jax.random.randint(part_splits[7], (KEPT,), 0, NA), jax.random.fold_in(part_splits[7], 1), 0, NA - 1).astype(jnp.int32),
        "kept_cols": set_ends(jax.random.randint(part_splits[8], (KEPT,), 0, BLOCK * BLOCK), jax.random.fold_in(part_splits[8], 1), 0, (BLOCK * BLOCK) - 1).astype(jnp.int32),
    }


def parity_sign(row_index, col_index):
    common_bits = jnp.bitwise_and(row_index, col_index)
    parity_sum = jnp.zeros_like(common_bits)
    for position in range(BLOCK.bit_length() - 1):
        parity_sum = parity_sum + jnp.bitwise_and(jnp.right_shift(common_bits, position), 1)
    return (1 - 2 * jnp.bitwise_and(parity_sum, 1)).astype(jnp.float32) / math.sqrt(BLOCK)

def hadamard_table():
    row_index = lax.broadcasted_iota(jnp.int32, (BLOCK, BLOCK), 0)
    col_index = lax.broadcasted_iota(jnp.int32, (BLOCK, BLOCK), 1)
    return parity_sign(row_index, col_index)

def reference(activations, curvature, vector_now, vector_before, sign_bits, prior_precision, beta_before, kept_rows, kept_cols):
    vector_half = vector_now.astype(jnp.bfloat16)
    act_groups = activations.reshape(TOKENS, N_FLAT, FF // N_FLAT).transpose(1, 0, 2)
    vec_groups = vector_half.reshape(N_FLAT, FF // N_FLAT, D)

    def add_group(running, pieces):
        term = jnp.dot(pieces[0], pieces[1], preferred_element_type=jnp.float32)
        rounded = lax.optimization_barrier(term.astype(jnp.bfloat16))
        return (running + rounded.astype(jnp.float32), None)
    outputs = lax.scan(add_group, jnp.zeros((TOKENS, D), jnp.float32), (act_groups, vec_groups))[0]
    scaled = (curvature[:, None] * outputs / TOKENS).astype(jnp.bfloat16)
    act_blocks = activations.reshape(N_DP, TOK_DEV, FF)
    scaled_blocks = scaled.reshape(N_DP, TOK_DEV, D)

    def add_block(running, pieces):
        term = lax.dot_general(pieces[0], pieces[1], (((0,), (0,)), ((), ())), preferred_element_type=jnp.float32)
        rounded = lax.optimization_barrier(term.astype(jnp.bfloat16))
        return (running + rounded.astype(jnp.float32), None)
    image_data = lax.scan(add_block, jnp.zeros((FF, D), jnp.float32), (act_blocks, scaled_blocks))[0]
    new_image = image_data + prior_precision[0] * vector_now
    alpha_value = jnp.mean(new_image * vector_now)
    residual = new_image - alpha_value * vector_now - beta_before[0] * vector_before
    beta_value = jnp.sqrt(jnp.mean(residual * residual) + 1e-06)
    vector_next = residual / beta_value
    signed = (2 * sign_bits - 1).astype(jnp.float32) * vector_next
    hadamard = hadamard_table()
    section_one = jnp.dot(signed.reshape(-1, BLOCK), hadamard, precision=lax.Precision.HIGHEST)
    section_one = section_one.reshape(NA // BLOCK, BLOCK, BLOCK * BLOCK)
    section_two = jnp.einsum('ri,bic->brc', hadamard, section_one, precision=lax.Precision.HIGHEST)
    section_two = section_two.reshape(NA, BLOCK * BLOCK)
    sketch = section_two[kept_rows, kept_cols]
    return (vector_next, alpha_value.reshape(1), beta_value.reshape(1), sketch)
```

```python
import math

import jax
import jax.numpy as jnp
from jax import lax
from jax.experimental import pallas as pl
from jax.experimental.pallas import tpu as pltpu
from jax.sharding import PartitionSpec as P

BLOCK = 128


def parity_sign(row_index, col_index):
    common_bits = jnp.bitwise_and(row_index, col_index)
    parity_sum = jnp.zeros_like(common_bits)
    for position in range(BLOCK.bit_length() - 1):
        parity_sum = parity_sum + jnp.bitwise_and(jnp.right_shift(common_bits, position), 1)
    return (1 - 2 * jnp.bitwise_and(parity_sum, 1)).astype(jnp.float32) / math.sqrt(BLOCK)


def hadamard_table():
    row_index = lax.broadcasted_iota(jnp.int32, (BLOCK, BLOCK), 0)
    col_index = lax.broadcasted_iota(jnp.int32, (BLOCK, BLOCK), 1)
    return parity_sign(row_index, col_index)


def pick_dense(column_block, hadamard, own_index, kept_rows, kept_cols):
    cols_here = column_block.shape[1]
    section_two = jnp.einsum(
        "ri,bic->brc",
        hadamard,
        column_block.reshape(-1, BLOCK, cols_here),
        precision=lax.Precision.HIGHEST,
    )
    section_two = section_two.reshape(-1, cols_here)
    first_col = own_index * cols_here
    inside = jnp.logical_and(kept_cols >= first_col, kept_cols < first_col + cols_here)
    local_col = jnp.clip(kept_cols - first_col, 0, cols_here - 1)
    return jnp.where(inside, section_two[kept_rows, local_col], 0.0)


def plain_on_device(
    activations,
    curvature,
    vector_now,
    vector_before,
    sign_bits,
    prior_precision,
    beta_before,
    kept_rows,
    kept_cols,
):
    token_count = activations.shape[0]
    out_width = vector_now.shape[1]
    local_rows = vector_now.shape[0]
    flat_count = lax.axis_size("flat")
    data_count = lax.axis_size("dp")
    total_tokens = token_count * data_count
    total_cells = local_rows * out_width * flat_count * data_count
    vector_half = vector_now.astype(jnp.bfloat16)
    columns = activations
    partial_out = jnp.dot(
        columns,
        lax.all_gather(vector_half, "dp", axis=0, tiled=True),
        preferred_element_type=jnp.float32,
    )
    shares = lax.psum_scatter(
        partial_out.astype(jnp.bfloat16), "flat", scatter_dimension=1, tiled=True
    ).astype(jnp.float32)
    scaled_share = (curvature[:, None] * shares / total_tokens).astype(jnp.bfloat16)
    scaled = lax.all_gather(scaled_share, "flat", axis=1, tiled=True)
    columns = activations
    image_data = lax.psum_scatter(
        lax.dot_general(
            columns, scaled, (((0,), (0,)), ((), ())), preferred_element_type=jnp.float32
        ).astype(jnp.bfloat16),
        "dp",
        scatter_dimension=0,
        tiled=True,
    ).astype(jnp.float32)
    new_image = image_data + prior_precision[0] * vector_now
    beta_old = beta_before[0]
    alpha_value = lax.psum(jnp.sum(new_image * vector_now), ("flat", "dp")) / total_cells
    residual = new_image - alpha_value * vector_now - beta_old * vector_before
    square = lax.psum(jnp.sum(residual * residual), ("flat", "dp")) / total_cells
    beta_value = jnp.sqrt(square + 1e-06)
    vector_next = residual / beta_value
    hadamard = hadamard_table()
    signed = (2 * sign_bits - 1).astype(jnp.float32) * vector_next
    rows_here = local_rows * out_width // (BLOCK * BLOCK)
    section_one = jnp.dot(signed.reshape(-1, BLOCK), hadamard, precision=lax.Precision.HIGHEST)
    section_one = section_one.reshape(rows_here, BLOCK * BLOCK)
    own_index = lax.axis_index(("flat", "dp"))
    column_block = lax.all_to_all(
        section_one.astype(jnp.bfloat16), ("flat", "dp"), split_axis=1, concat_axis=0, tiled=True
    ).astype(section_one.dtype)
    local_values = pick_dense(column_block, hadamard, own_index, kept_rows, kept_cols)
    sketch = lax.psum(local_values, ("flat", "dp"))
    return (vector_next, alpha_value.reshape(1), beta_value.reshape(1), sketch)


def residual_kernel(scalars, n_ref, v_ref, b_ref, s_ref, r_ref, x_ref, sq_ref):
    @pl.when(pl.program_id(0) == 0)
    def _():
        sq_ref[...] = jnp.zeros_like(sq_ref)

    rows, width = n_ref.shape
    residual = n_ref[...] - scalars[0] * v_ref[...] - scalars[1] * b_ref[...]
    r_ref[...] = residual
    signs = (2 * s_ref[...] - 1).astype(jnp.float32)
    x_ref[...] = (signs * residual).astype(jnp.bfloat16)
    square = jnp.sum((residual * residual).reshape(rows // 8, 8, width), axis=0)
    total = square[:, :128]
    for k in range(1, width // 128):
        total = total + square[:, k * 128 : (k + 1) * 128]
    sq_ref[...] += total


def residual_pass(scalars, image, vector_now, vector_before, sign_bits):
    rows, width = image.shape
    tile = 64
    block = pl.BlockSpec((tile, width), lambda i: (i, 0))
    return pl.pallas_call(
        residual_kernel,
        grid=(rows // tile,),
        out_shape=(
            jax.ShapeDtypeStruct((rows, width), jnp.float32),
            jax.ShapeDtypeStruct((rows, width), jnp.bfloat16),
            jax.ShapeDtypeStruct((8, 128), jnp.float32),
        ),
        in_specs=[pl.BlockSpec(memory_space=pltpu.SMEM)] + [block] * 4,
        out_specs=(block, block, pl.BlockSpec((8, 128), lambda i: (0, 0))),
        compiler_params=pltpu.CompilerParams(vmem_limit_bytes=40 * 2**20),
    )(scalars, image, vector_now, vector_before, sign_bits)


def odd_bits(common):
    common = common ^ (common >> 4)
    common = common ^ (common >> 2)
    common = common ^ (common >> 1)
    return common & 1


def sketch_kernel(first_ref, x_ref, row_ref, col_ref, out_ref):
    rows, width = x_ref.shape
    count = row_ref.shape[0]
    per_row = BLOCK * BLOCK // width
    kept_row, kept_col = row_ref[...], col_ref[...]
    place = lax.broadcasted_iota(jnp.int32, (count, rows), 1)
    row = first_ref[0] + place // per_row
    here = jnp.logical_and(row // BLOCK == kept_row // BLOCK, place % per_row == kept_col // width)
    sign = 1 - 2 * odd_bits((row % BLOCK) & (kept_row % BLOCK))
    weights = jnp.where(here, sign, 0).astype(jnp.float32).astype(jnp.bfloat16)
    group = (kept_col % width) // BLOCK
    span = 512
    total = jnp.zeros((count, BLOCK), jnp.float32)
    for k in range(width // span):
        sums = jnp.dot(
            weights, x_ref[:, k * span : (k + 1) * span], preferred_element_type=jnp.float32
        )
        for g in range(span // BLOCK):
            total = jnp.where(
                group == k * (span // BLOCK) + g, sums[:, g * BLOCK : (g + 1) * BLOCK], total
            )
    lane = lax.broadcasted_iota(jnp.int32, (count, BLOCK), 1)
    sign = (1 - 2 * odd_bits(lane & (kept_col % BLOCK))).astype(jnp.float32)
    out_ref[...] = jnp.sum(total * sign, axis=1, keepdims=True) / BLOCK


def sketch_pass(first_row, signed, kept_rows, kept_cols):
    rows, width = signed.shape
    kept = kept_rows.shape[0]
    tile = 256
    narrow = pl.BlockSpec((tile, 1), lambda i: (i, 0))
    return pl.pallas_call(
        sketch_kernel,
        grid=(kept // tile,),
        out_shape=jax.ShapeDtypeStruct((kept, 1), jnp.float32),
        in_specs=[
            pl.BlockSpec(memory_space=pltpu.SMEM),
            pl.BlockSpec((rows, width), lambda i: (0, 0)),
            narrow,
            narrow,
        ],
        out_specs=narrow,
        compiler_params=pltpu.CompilerParams(vmem_limit_bytes=40 * 2**20),
    )(first_row, signed, kept_rows.reshape(kept, 1), kept_cols.reshape(kept, 1))


def on_device(
    activations,
    curvature,
    vector_now,
    vector_before,
    sign_bits,
    prior_precision,
    beta_before,
    kept_rows,
    kept_cols,
):
    flat_count = lax.axis_size("flat")
    data_count = lax.axis_size("dp")
    rows, width = vector_now.shape
    total_cells = rows * width * flat_count * data_count
    tokens = activations.shape[0] * data_count
    columns = lax.all_to_all(activations, "dp", split_axis=1, concat_axis=0, tiled=True)
    outputs = jnp.dot(
        columns, vector_now.astype(jnp.bfloat16), preferred_element_type=jnp.float32
    ).astype(jnp.bfloat16)
    shares = lax.psum_scatter(outputs, "dp", scatter_dimension=0, tiled=True)
    shares = lax.psum_scatter(shares, "flat", scatter_dimension=1, tiled=True).astype(jnp.float32)
    scaled = (curvature[:, None] * shares / tokens).astype(jnp.bfloat16)
    scaled = lax.all_gather(scaled, "flat", axis=1, tiled=True)
    scaled = lax.all_gather(scaled, "dp", axis=0, tiled=True)
    image = jnp.dot(columns.T, scaled, preferred_element_type=jnp.float32)
    image = image + prior_precision[0] * vector_now
    alpha_value = lax.psum(jnp.sum(image * vector_now), ("flat", "dp")).reshape(1) / total_cells
    residual, signed, square = residual_pass(
        jnp.concatenate([alpha_value, beta_before]), image, vector_now, vector_before, sign_bits
    )
    own_index = lax.axis_index(("flat", "dp"))
    first_row = (own_index * (rows * width // (BLOCK * BLOCK))).reshape(1)
    local_values = sketch_pass(first_row, signed, kept_rows, kept_cols)
    kept = kept_rows.shape[0]
    sums = lax.psum(
        jnp.concatenate([local_values.reshape(kept // 128, 128), square]), ("flat", "dp")
    )
    beta_value = jnp.sqrt(jnp.sum(sums[kept // 128 :]) / total_cells + 1e-06)
    vector_next = residual / beta_value
    sketch = sums[: kept // 128].reshape(kept) / beta_value
    return (vector_next, alpha_value, beta_value.reshape(1), sketch)


def fits(mesh):
    return mesh.shape["dp"] == 4 and mesh.shape["flat"] == 4


def solution(mesh):
    placed = (
        P(("groups", "dp"), "flat"),
        P(("groups", "dp")),
        P(("groups", "flat", "dp"), None),
        P(("groups", "flat", "dp"), None),
        P(("groups", "flat", "dp"), None),
        P("groups"),
        P("groups"),
        P("groups"),
        P("groups"),
    )
    return jax.shard_map(
        on_device if fits(mesh) else plain_on_device,
        mesh=mesh,
        in_specs=placed,
        out_specs=(P(("groups", "flat", "dp"), None), P("groups"), P("groups"), P("groups")),
        check_vma=False,
    )
```

```python
import math

import jax
import jax.numpy as jnp
from jax import lax
from jax.experimental import pallas as pl
from jax.experimental.pallas import tpu as pltpu
from jax.sharding import PartitionSpec as P

BLOCK = 128


def parity_sign(row_index, col_index):
    common_bits = jnp.bitwise_and(row_index, col_index)
    parity_sum = jnp.zeros_like(common_bits)
    for position in range(BLOCK.bit_length() - 1):
        parity_sum = parity_sum + jnp.bitwise_and(jnp.right_shift(common_bits, position), 1)
    return (1 - 2 * jnp.bitwise_and(parity_sum, 1)).astype(jnp.float32) / math.sqrt(BLOCK)


def hadamard_table():
    row_index = lax.broadcasted_iota(jnp.int32, (BLOCK, BLOCK), 0)
    col_index = lax.broadcasted_iota(jnp.int32, (BLOCK, BLOCK), 1)
    return parity_sign(row_index, col_index)


def pick_dense(column_block, hadamard, own_index, kept_rows, kept_cols):
    cols_here = column_block.shape[1]
    section_two = jnp.einsum(
        "ri,bic->brc",
        hadamard,
        column_block.reshape(-1, BLOCK, cols_here),
        precision=lax.Precision.HIGHEST,
    )
    section_two = section_two.reshape(-1, cols_here)
    first_col = own_index * cols_here
    inside = jnp.logical_and(kept_cols >= first_col, kept_cols < first_col + cols_here)
    local_col = jnp.clip(kept_cols - first_col, 0, cols_here - 1)
    return jnp.where(inside, section_two[kept_rows, local_col], 0.0)


def plain_on_device(
    activations,
    curvature,
    vector_now,
    vector_before,
    sign_bits,
    prior_precision,
    beta_before,
    kept_rows,
    kept_cols,
):
    token_count = activations.shape[0]
    out_width = vector_now.shape[1]
    local_rows = vector_now.shape[0]
    flat_count = lax.axis_size("flat")
    data_count = lax.axis_size("dp")
    total_tokens = token_count * data_count
    total_cells = local_rows * out_width * flat_count * data_count
    vector_half = vector_now.astype(jnp.bfloat16)
    columns = activations
    partial_out = jnp.dot(
        columns,
        lax.all_gather(vector_half, "dp", axis=0, tiled=True),
        preferred_element_type=jnp.float32,
    )
    shares = lax.psum_scatter(
        partial_out.astype(jnp.bfloat16), "flat", scatter_dimension=1, tiled=True
    ).astype(jnp.float32)
    scaled_share = (curvature[:, None] * shares / total_tokens).astype(jnp.bfloat16)
    scaled = lax.all_gather(scaled_share, "flat", axis=1, tiled=True)
    columns = activations
    image_data = lax.psum_scatter(
        lax.dot_general(
            columns, scaled, (((0,), (0,)), ((), ())), preferred_element_type=jnp.float32
        ).astype(jnp.bfloat16),
        "dp",
        scatter_dimension=0,
        tiled=True,
    ).astype(jnp.float32)
    new_image = image_data + prior_precision[0] * vector_now
    beta_old = beta_before[0]
    alpha_value = lax.psum(jnp.sum(new_image * vector_now), ("flat", "dp")) / total_cells
    residual = new_image - alpha_value * vector_now - beta_old * vector_before
    square = lax.psum(jnp.sum(residual * residual), ("flat", "dp")) / total_cells
    beta_value = jnp.sqrt(square + 1e-06)
    vector_next = residual / beta_value
    hadamard = hadamard_table()
    signed = (2 * sign_bits - 1).astype(jnp.float32) * vector_next
    rows_here = local_rows * out_width // (BLOCK * BLOCK)
    section_one = jnp.dot(signed.reshape(-1, BLOCK), hadamard, precision=lax.Precision.HIGHEST)
    section_one = section_one.reshape(rows_here, BLOCK * BLOCK)
    own_index = lax.axis_index(("flat", "dp"))
    column_block = lax.all_to_all(
        section_one.astype(jnp.bfloat16), ("flat", "dp"), split_axis=1, concat_axis=0, tiled=True
    ).astype(section_one.dtype)
    local_values = pick_dense(column_block, hadamard, own_index, kept_rows, kept_cols)
    sketch = lax.psum(local_values, ("flat", "dp"))
    return (vector_next, alpha_value.reshape(1), beta_value.reshape(1), sketch)


def residual_kernel(scalars, v_ref, b_ref, s_ref, *refs):
    n_refs, (r_ref, x_ref, sq_ref) = refs[:-3], refs[-3:]

    @pl.when(pl.program_id(0) == 0)
    def _():
        sq_ref[...] = jnp.zeros_like(sq_ref)

    rows, width = v_ref.shape
    image = jnp.concatenate([ref[...] for ref in n_refs], axis=1)
    residual = image - scalars[0] * v_ref[...] - scalars[1] * b_ref[...]
    r_ref[...] = residual
    signs = (2 * s_ref[...] - 1).astype(jnp.float32)
    x_ref[...] = (signs * residual).astype(jnp.bfloat16)
    square = jnp.sum((residual * residual).reshape(rows // 8, 8, width), axis=0)
    total = square[:, :128]
    for k in range(1, width // 128):
        total = total + square[:, k * 128 : (k + 1) * 128]
    sq_ref[...] += total


def residual_pass(scalars, images, vector_now, vector_before, sign_bits):
    rows, width = vector_now.shape
    tile = 64
    narrow = pl.BlockSpec((tile, images[0].shape[1]), lambda i: (i, 0))
    block = pl.BlockSpec((tile, width), lambda i: (i, 0))
    return pl.pallas_call(
        residual_kernel,
        grid=(rows // tile,),
        out_shape=(
            jax.ShapeDtypeStruct((rows, width), jnp.float32),
            jax.ShapeDtypeStruct((rows, width), jnp.bfloat16),
            jax.ShapeDtypeStruct((8, 128), jnp.float32),
        ),
        in_specs=[pl.BlockSpec(memory_space=pltpu.SMEM)] + [block] * 3 + [narrow] * len(images),
        out_specs=(block, block, pl.BlockSpec((8, 128), lambda i: (0, 0))),
        compiler_params=pltpu.CompilerParams(vmem_limit_bytes=40 * 2**20),
    )(scalars, vector_now, vector_before, sign_bits, *images)


def odd_bits(common):
    common = common ^ (common >> 4)
    common = common ^ (common >> 2)
    common = common ^ (common >> 1)
    return common & 1


def sketch_kernel(first_ref, x_ref, row_ref, col_ref, out_ref):
    rows, width = x_ref.shape
    count = row_ref.shape[0]
    per_row = BLOCK * BLOCK // width
    kept_row, kept_col = row_ref[...], col_ref[...]
    place = lax.broadcasted_iota(jnp.int32, (count, rows), 1)
    row = first_ref[0] + place // per_row
    here = jnp.logical_and(row // BLOCK == kept_row // BLOCK, place % per_row == kept_col // width)
    sign = 1 - 2 * odd_bits((row % BLOCK) & (kept_row % BLOCK))
    weights = jnp.where(here, sign, 0).astype(jnp.float32).astype(jnp.bfloat16)
    group = (kept_col % width) // BLOCK
    span = 512
    total = jnp.zeros((count, BLOCK), jnp.float32)
    for k in range(width // span):
        sums = jnp.dot(
            weights, x_ref[:, k * span : (k + 1) * span], preferred_element_type=jnp.float32
        )
        for g in range(span // BLOCK):
            total = jnp.where(
                group == k * (span // BLOCK) + g, sums[:, g * BLOCK : (g + 1) * BLOCK], total
            )
    lane = lax.broadcasted_iota(jnp.int32, (count, BLOCK), 1)
    sign = (1 - 2 * odd_bits(lane & (kept_col % BLOCK))).astype(jnp.float32)
    out_ref[...] = jnp.sum(total * sign, axis=1, keepdims=True) / BLOCK


def sketch_pass(first_row, signed, kept_rows, kept_cols):
    rows, width = signed.shape
    kept = kept_rows.shape[0]
    tile = 256
    narrow = pl.BlockSpec((tile, 1), lambda i: (i, 0))
    return pl.pallas_call(
        sketch_kernel,
        grid=(kept // tile,),
        out_shape=jax.ShapeDtypeStruct((kept, 1), jnp.float32),
        in_specs=[
            pl.BlockSpec(memory_space=pltpu.SMEM),
            pl.BlockSpec((rows, width), lambda i: (0, 0)),
            narrow,
            narrow,
        ],
        out_specs=narrow,
        compiler_params=pltpu.CompilerParams(vmem_limit_bytes=40 * 2**20),
    )(first_row, signed, kept_rows.reshape(kept, 1), kept_cols.reshape(kept, 1))


def on_device(
    activations,
    curvature,
    vector_now,
    vector_before,
    sign_bits,
    prior_precision,
    beta_before,
    kept_rows,
    kept_cols,
):
    flat_count = lax.axis_size("flat")
    data_count = lax.axis_size("dp")
    rows, width = vector_now.shape
    total_cells = rows * width * flat_count * data_count
    tok = activations.shape[0]
    tokens = tok * data_count
    part = tok // flat_count
    place, own = lax.axis_index("flat"), lax.axis_index("dp")
    levels = [1 << k for k in range(data_count.bit_length() - 1)]
    masks = [0]
    for mask in reversed(levels):
        masks = masks + [mask ^ one for one in masks]

    def swap(block, mask):
        return lax.ppermute(block, "dp", [(i, i ^ mask) for i in range(data_count)])

    def shift(block, by):
        return lax.ppermute(block, "flat", [(i, (i + by) % flat_count) for i in range(flat_count)])

    parts = activations.reshape(flat_count, part, -1)
    back = parts[::-1]
    turned = lax.dynamic_slice_in_dim(
        jnp.concatenate([back, back]), flat_count - 1 - place, flat_count, 0
    ).reshape(tok, -1)
    weight = lax.dynamic_slice(curvature, (place * part,), (part,))[:, None]
    pieces = []
    for mask in masks:
        piece = lax.dynamic_slice(turned, (0, (own ^ mask) * rows), (tok, rows))
        pieces.append(swap(piece, mask) if mask else piece)
    columns = jnp.concatenate(pieces, axis=0)
    half = vector_now.astype(jnp.bfloat16)
    chunk = width // 4
    images = []
    inner = jnp.float32(0)

    def add(left, right):
        return (left.astype(jnp.float32) + right.astype(jnp.float32)).astype(jnp.bfloat16)

    for c in range(width // chunk):
        cols = slice(c * chunk, (c + 1) * chunk)
        held = jnp.dot(columns, half[:, cols], preferred_element_type=jnp.float32)
        held = held.astype(jnp.bfloat16)
        for mask in levels:
            middle = held.shape[0] // 2
            held = add(held[:middle], swap(held[middle:], mask))
        total = held[:part].astype(jnp.float32)
        for j in range(1, flat_count):
            total = total + shift(held[j * part : (j + 1) * part], -j).astype(jnp.float32)
        scaled = (weight * total / tokens).astype(jnp.bfloat16)
        scaled = jnp.concatenate([scaled] + [shift(scaled, j) for j in range(1, flat_count)])
        for mask in reversed(levels):
            scaled = jnp.concatenate([scaled, swap(scaled, mask)])
        image = jnp.dot(columns.T, scaled, preferred_element_type=jnp.float32)
        image = image + prior_precision[0] * vector_now[:, cols]
        inner = inner + jnp.sum(image * vector_now[:, cols])
        images.append(image)
    alpha_value = lax.psum(inner, ("flat", "dp")).reshape(1) / total_cells
    residual, signed, square = residual_pass(
        jnp.concatenate([alpha_value, beta_before]), images, vector_now, vector_before, sign_bits
    )
    own_index = lax.axis_index(("flat", "dp"))
    first_row = (own_index * (rows * width // (BLOCK * BLOCK))).reshape(1)
    local_values = sketch_pass(first_row, signed, kept_rows, kept_cols)
    kept = kept_rows.shape[0]
    sums = lax.psum(
        jnp.concatenate([local_values.reshape(kept // 128, 128), square]), ("flat", "dp")
    )
    beta_value = jnp.sqrt(jnp.sum(sums[kept // 128 :]) / total_cells + 1e-06)
    vector_next = residual / beta_value
    sketch = sums[: kept // 128].reshape(kept) / beta_value
    return (vector_next, alpha_value, beta_value.reshape(1), sketch)


def fits(mesh):
    return mesh.shape["dp"] == 4 and mesh.shape["flat"] == 4


def solution(mesh):
    placed = (
        P(("groups", "dp"), "flat"),
        P(("groups", "dp")),
        P(("groups", "flat", "dp"), None),
        P(("groups", "flat", "dp"), None),
        P(("groups", "flat", "dp"), None),
        P("groups"),
        P("groups"),
        P("groups"),
        P("groups"),
    )
    return jax.shard_map(
        on_device if fits(mesh) else plain_on_device,
        mesh=mesh,
        in_specs=placed,
        out_specs=(P(("groups", "flat", "dp"), None), P("groups"), P("groups"), P("groups")),
        check_vma=False,
    )
```
